32 devices in a mesh: rows: 4 (over y, core), modes: 8 (over z, x).
Axes of the slice: x: 2, y: 2, z: 4, core: 2. Of those that a mesh axis runs over, the one named last changes fastest.
Arguments:
- transfer: float32 [16384, 16384], P('rows', 'modes'), may hold values from -1 to 1
- observed: float32 [32, 16384], P('modes', 'rows'), may hold values from -6 to 6
- start: float32 [32, 16384], P('rows', 'modes'), may hold values from -6 to 6
- probe: bfloat16 [32, 16384], P(('rows', 'modes')), may hold values from -6 to 6
- w_first: bfloat16 [9, 48, 2], replicated, may hold values from -1.5 to 1.5
- w_mid: bfloat16 [9, 48, 48], replicated, may hold values from -0.3125 to 0.3125
- w_last: bfloat16 [9, 1, 48], replicated, may hold values from -0.3125 to 0.3125
Outputs:
- recovered: float32 [32, 16384], P(('rows', 'modes'))
The draws below stay inside these ranges and needn't reach their ends.
All inputs are finite; a program needn't handle non-finite values.
Results may differ from the reference program's by a relative error of at most 0.0049.
Values sent between devices are 32-bit elements; how exact they have to be, the bound alone decides.
A program may use at most 128 MiB of HBM per device.

```python
import jax
import jax.numpy as jnp
from jax import lax

DET = 16384
IMG = 128
CH = 48
ITERS = 2
PIX = 16384
FRAMES = 32


def draw_transfer(key, part):
    key_entries, key_rows, key_cols = jax.random.split(key, 3)
    row_pos = jnp.arange(DET, dtype=jnp.float32) / DET
    col_pos = jnp.arange(PIX, dtype=jnp.float32) / PIX
    raw_entries = jnp.clip(jax.random.normal(key_entries, (DET, PIX), jnp.float32), -4.0, 4.0)
    row_scale = jnp.exp(jax.random.uniform(key_rows, (DET,), jnp.float32, -1.151, 1.151))
    col_scale = jnp.exp(jax.random.uniform(key_cols, (PIX,), jnp.float32, -1.151, 1.151))
    row_scale = row_scale * jnp.sqrt(1.0 + 2.0 * row_pos)
    col_scale = col_scale * jnp.sqrt(1.0 + 2.0 * col_pos)
    return raw_entries * row_scale[:, None] * col_scale[None, :] / IMG


def shard_levels(own_key, shape, pieces, low, top_value):
    level, own = 1.0, jax.random.fold_in(own_key, 6)
    for dim, parts in pieces:
        steps = jnp.exp(jax.random.uniform(jax.random.fold_in(own, dim), (parts,), jnp.float32, low / len(pieces), top_value / len(pieces)))
        level = level * jnp.repeat(steps, shape[dim] // parts).reshape([-1 if axis == dim else 1 for axis in range(len(shape))])
    return level


def noise(key, shape, width, limit, cuts=(), kind=jnp.bfloat16):
    factor_of = shard_levels(key, shape, cuts, -0.22, 0.18) if cuts else 1.0
    values = jax.random.normal(key, shape, jnp.float32) * width * factor_of
    return jnp.minimum(jnp.maximum(values, -limit), limit).astype(kind)


def setup_inputs(seed: int = 0) -> dict:
    streams_of = jax.random.split(jax.random.key(seed), 8)
    return {
        "transfer": draw_transfer(jax.random.fold_in(streams_of[7], 71), 0),
        "observed": noise(streams_of[1], (FRAMES, DET), 1.0, 6.0, ((0, 8), (1, 4)), jnp.float32),
        "start": noise(streams_of[2], (FRAMES, PIX), 1.0, 6.0, ((0, 4), (1, 8)), jnp.float32),
        "probe": noise(streams_of[3], (FRAMES, PIX), 1.0, 6.0, ((0, 32),)),
        "w_first": noise(streams_of[4], (9, CH, 2), 18 ** -0.5, 1.5),
        "w_mid": noise(streams_of[5], (9, CH, CH), (9 * CH) ** -0.5, 0.3125),
        "w_last": noise(streams_of[6], (9, 1, CH), (9 * CH) ** -0.5, 0.3125),
    }


def conv_layer(weights, feature):
    extent_rows, extent_cols = (feature.shape[1], feature.shape[2])
    padded = jnp.pad(feature.astype(jnp.float32), ((0, 0), (1, 1), (1, 1)))
    summed = jnp.zeros((weights.shape[1], extent_rows, extent_cols), jnp.float32)
    for offset in range(9):
        row_shift = offset // 3
        col_shift = offset % 3
        window = padded[:, row_shift:row_shift + extent_rows, col_shift:col_shift + extent_cols]
        summed = summed + jnp.einsum('oc,chw->ohw', weights[offset].astype(jnp.float32), window, precision=lax.Precision.HIGHEST)
    return summed

def silu_slope(values):
    logistic = jax.nn.sigmoid(values)
    return logistic * (1.0 + values * (1.0 - logistic))

def denoise(bundle, w_first, w_mid, w_last):
    pushed_one, levels_one, probe_one = bundle
    picture = pushed_one.reshape(IMG, IMG)
    stacked = jnp.stack([picture, jnp.zeros_like(picture) + levels_one]).astype(jnp.bfloat16)
    first_pre = conv_layer(w_first, stacked)
    first_tan = conv_layer(w_first[:, :, 0:1], probe_one.reshape(1, IMG, IMG))
    active_one = jax.nn.silu(first_pre).astype(jnp.bfloat16)
    tan_one = (silu_slope(first_pre) * first_tan).astype(jnp.bfloat16)
    second_pre = conv_layer(w_mid, active_one)
    second_tan = conv_layer(w_mid, tan_one)
    active_two = jax.nn.silu(second_pre).astype(jnp.bfloat16)
    tan_two = (silu_slope(second_pre) * second_tan).astype(jnp.bfloat16)
    out_pre = conv_layer(w_last, active_two).reshape(-1)
    out_tan = conv_layer(w_last, tan_two).reshape(-1)
    denoised = pushed_one - out_pre
    probe_vals = probe_one.astype(jnp.float32)
    spread = jnp.mean(probe_vals * (probe_vals - out_tan))
    return (denoised, spread)

def reference(transfer, observed, start, probe, w_first, w_mid, w_last):
    trace = jnp.sum(transfer * transfer)
    estimate = start
    for iteration in range(ITERS):
        fitted = jnp.dot(estimate, transfer.T, precision=lax.Precision.HIGHEST, preferred_element_type=jnp.float32)
        misfit = observed - fitted
        squares = lax.optimization_barrier(jnp.sum(misfit * misfit, axis=1))
        levels = jnp.sqrt(squares / trace)
        back_sum = jnp.dot(misfit, transfer, precision=lax.Precision.HIGHEST, preferred_element_type=jnp.float32)
        pushed = estimate + PIX / trace * back_sum
        denoised, spread = lax.map(lambda bundle: denoise(bundle, w_first, w_mid, w_last), (pushed, levels, probe))
        onsager = denoised - spread[:, None] * pushed
        gains = lax.optimization_barrier(jnp.sum(denoised * onsager, axis=1)) / (lax.optimization_barrier(jnp.sum(onsager * onsager, axis=1)) + 1e-06)
        estimate = gains[:, None] * onsager
    return estimate
```

```python
import functools

import jax
import jax.numpy as jnp
from jax import lax
from jax.experimental import pallas as pl
from jax.experimental.pallas import tpu as pltpu
from jax.sharding import PartitionSpec as P

IMG = 128
ITERS = 2
PIX = 16384
EXTRA = 128
VMEM_BYTES = 56 * 1024 * 1024


def exchange_kernel(axis, count, gather, x_ref, o_ref, send_sem, recv_sem, local_sem):
    me = lax.axis_index(axis)
    barrier = pltpu.get_barrier_semaphore()
    for step in range(1, count):
        pl.semaphore_signal(
            barrier,
            inc=1,
            device_id={axis: lax.rem(me + step, count)},
            device_id_type=pl.DeviceIdType.MESH,
        )
    pl.semaphore_wait(barrier, count - 1)
    copies = []
    for step in range(1, count):
        peer = lax.rem(me + step, count)
        copy = pltpu.make_async_remote_copy(
            src_ref=x_ref if gather else x_ref.at[peer],
            dst_ref=o_ref.at[me],
            send_sem=send_sem.at[step],
            recv_sem=recv_sem.at[step],
            device_id={axis: peer},
            device_id_type=pl.DeviceIdType.MESH,
        )
        copy.start()
        copies.append(copy)
    own = pltpu.make_async_copy(x_ref if gather else x_ref.at[me], o_ref.at[me], local_sem)
    own.start()
    own.wait()
    for copy in copies:
        copy.wait()


def exchange(block, axis, count, ident, gather=False):
    shape = (count,) + block.shape if gather else block.shape
    return pl.pallas_call(
        functools.partial(exchange_kernel, axis, count, gather),
        out_shape=jax.ShapeDtypeStruct(shape, jnp.float32),
        in_specs=[pl.BlockSpec(memory_space=pltpu.VMEM)],
        out_specs=pl.BlockSpec(memory_space=pltpu.VMEM),
        scratch_shapes=[
            pltpu.SemaphoreType.DMA((count,)),
            pltpu.SemaphoreType.DMA((count,)),
            pltpu.SemaphoreType.DMA,
        ],
        compiler_params=pltpu.CompilerParams(
            collective_id=ident, has_side_effects=True, vmem_limit_bytes=VMEM_BYTES
        ),
        name="exchange_" + axis + str(ident),
    )(block)


def three_products(vectors, block, dims):
    count = vectors.shape[0]
    vector_high = vectors.astype(jnp.bfloat16)
    vector_low = (vectors - vector_high.astype(jnp.float32)).astype(jnp.bfloat16)
    vectors = jnp.concatenate([vector_high, vector_low], axis=0)
    high = block.astype(jnp.bfloat16)
    low = (block - high.astype(jnp.float32)).astype(jnp.bfloat16)
    both = lax.dot_general(vectors, high, (dims, ((), ())), preferred_element_type=jnp.float32)
    rest = lax.dot_general(
        vectors[:count], low, (dims, ((), ())), preferred_element_type=jnp.float32
    )
    return both[:count] + both[count:] + rest


def fit_kernel(vectors_ref, transfer_ref, fit_ref, trace_ref):
    block = transfer_ref[...]
    fit_ref[...] = three_products(vectors_ref[...], block, ((1,), (1,)))

    @pl.when(pl.program_id(0) == 0)
    def _():
        trace_ref[...] = jnp.zeros_like(trace_ref)

    rows, cols = block.shape
    trace_ref[...] += jnp.sum((block * block).reshape(rows // 8, 8, cols), axis=0)


def fit_only_kernel(vectors_ref, transfer_ref, fit_ref):
    fit_ref[...] = three_products(vectors_ref[...], transfer_ref[...], ((1,), (1,)))


def fit(vectors, transfer, with_trace):
    rows, cols = transfer.shape
    tile = min(512, rows)
    count = vectors.shape[0]
    out_specs = [pl.BlockSpec((count, tile), lambda i: (0, i))]
    out_shape = [jax.ShapeDtypeStruct((count, rows), jnp.float32)]
    if with_trace:
        out_specs.append(pl.BlockSpec((8, cols), lambda i: (0, 0)))
        out_shape.append(jax.ShapeDtypeStruct((8, cols), jnp.float32))
    return pl.pallas_call(
        fit_kernel if with_trace else fit_only_kernel,
        grid=(rows // tile,),
        in_specs=[
            pl.BlockSpec((count, cols), lambda i: (0, 0)),
            pl.BlockSpec((tile, cols), lambda i: (i, 0)),
        ],
        out_specs=out_specs,
        out_shape=out_shape,
        compiler_params=pltpu.CompilerParams(vmem_limit_bytes=VMEM_BYTES),
        name="fit",
    )(vectors, transfer)


def adjoint_kernel(vectors_ref, transfer_ref, back_ref):
    @pl.when(pl.program_id(0) == 0)
    def _():
        back_ref[...] = jnp.zeros_like(back_ref)

    back_ref[...] += three_products(vectors_ref[...], transfer_ref[...], ((1,), (0,)))


def adjoint(vectors, transfer):
    rows, cols = transfer.shape
    tile = min(512, rows)
    count = vectors.shape[0]
    return pl.pallas_call(
        adjoint_kernel,
        grid=(rows // tile,),
        in_specs=[
            pl.BlockSpec((count, tile), lambda i: (0, i)),
            pl.BlockSpec((tile, cols), lambda i: (i, 0)),
        ],
        out_specs=pl.BlockSpec((count, cols), lambda i: (0, 0)),
        out_shape=jax.ShapeDtypeStruct((count, cols), jnp.float32),
        compiler_params=pltpu.CompilerParams(vmem_limit_bytes=VMEM_BYTES),
        name="adjoint",
    )(vectors, transfer)


def conv_layer(weights, feature):
    in_chan, extent_rows, extent_cols = feature.shape
    out_chan = weights.shape[1]
    padded = jnp.pad(feature, ((0, 0), (1, 1), (1, 1)))
    if out_chan == 1:
        taps_flat = weights[:, 0, :]
        products = jnp.dot(
            taps_flat,
            feature.reshape(in_chan, extent_rows * extent_cols),
            preferred_element_type=jnp.float32,
        )
        products = jnp.pad(products.reshape(9, extent_rows, extent_cols), ((0, 0), (1, 1), (1, 1)))
        summed = jnp.zeros((extent_rows, extent_cols), jnp.float32)
        for offset in range(9):
            row_shift = offset // 3
            col_shift = offset % 3
            summed = (
                summed
                + products[
                    offset, row_shift : row_shift + extent_rows, col_shift : col_shift + extent_cols
                ]
            )
        return summed.reshape(1, extent_rows, extent_cols)
    windows = []
    for offset in range(9):
        row_shift = offset // 3
        col_shift = offset % 3
        windows.append(
            padded[:, row_shift : row_shift + extent_rows, col_shift : col_shift + extent_cols]
        )
    columns = jnp.concatenate(windows, axis=0).reshape(9 * in_chan, extent_rows * extent_cols)
    weight_flat = jnp.transpose(weights, (1, 0, 2)).reshape(out_chan, 9 * in_chan)
    summed = jnp.dot(weight_flat, columns, preferred_element_type=jnp.float32)
    return summed.reshape(out_chan, extent_rows, extent_cols)


def silu_slope(values):
    logistic = jax.nn.sigmoid(values)
    return logistic * (1.0 + values * (1.0 - logistic))


def denoise(bundle, w_first, w_mid, w_last):
    pushed_one, levels_one, probe_one = bundle
    picture = pushed_one.reshape(IMG, IMG)
    stacked = jnp.stack([picture, jnp.zeros_like(picture) + levels_one]).astype(jnp.bfloat16)
    first_pre = conv_layer(w_first, stacked)
    first_tan = conv_layer(w_first[:, :, 0:1], probe_one.reshape(1, IMG, IMG))
    active_one = jax.nn.silu(first_pre).astype(jnp.bfloat16)
    tan_one = (silu_slope(first_pre) * first_tan).astype(jnp.bfloat16)
    second_pre = conv_layer(w_mid, active_one)
    second_tan = conv_layer(w_mid, tan_one)
    active_two = jax.nn.silu(second_pre).astype(jnp.bfloat16)
    tan_two = (silu_slope(second_pre) * second_tan).astype(jnp.bfloat16)
    out_pre = conv_layer(w_last, active_two).reshape(-1)
    out_tan = conv_layer(w_last, tan_two).reshape(-1)
    denoised = pushed_one - out_pre
    probe_vals = probe_one.astype(jnp.float32)
    spread = jnp.mean(probe_vals * (probe_vals - out_tan))
    return (denoised, spread)


def body(transfer, observed, start, probe, w_first, w_mid, w_last):
    row_count = lax.axis_size("rows")
    mode_count = lax.axis_size("modes")
    frames_dev = probe.shape[0]
    frames = frames_dev * row_count * mode_count
    per_row, per_mode = frames // row_count, frames // mode_count
    det_rows, cols = transfer.shape
    ident = 0
    estimate = start
    trace, recovered = None, None
    for iteration in range(ITERS):
        everyone = exchange(estimate, "rows", row_count, ident, gather=True).reshape(frames, cols)
        outs = fit(everyone, transfer, iteration == 0)
        partial_value = outs[0]
        if iteration == 0:
            partial_value = jnp.concatenate(
                [partial_value, jnp.full((frames, EXTRA), jnp.sum(outs[1]))], axis=1
            )
        summed = jnp.sum(
            exchange(
                partial_value.reshape(mode_count, per_mode, partial_value.shape[1]),
                "modes",
                mode_count,
                ident + 1,
            ),
            axis=0,
        )
        if iteration == 0:
            trace_rows = summed[0, det_rows]
        misfit = observed - summed[:, :det_rows]
        misfit_all = exchange(misfit, "modes", mode_count, ident + 2, gather=True)
        misfit_all = misfit_all.reshape(frames, det_rows)
        square_part = jnp.sum(misfit_all * misfit_all, axis=1, keepdims=True)
        back = adjoint(misfit_all, transfer)
        lane = lax.broadcasted_iota(jnp.int32, (frames, EXTRA), 1)
        back = jnp.concatenate(
            [back, jnp.where(lane == 0, square_part, trace_rows)], axis=1
        )
        back = jnp.sum(
            exchange(back.reshape(row_count, per_row, cols + EXTRA), "rows", row_count, ident + 3),
            axis=0,
        )
        if iteration == 0:
            trace = back[0, cols + 1]
        pushed_rows = jnp.concatenate(
            [estimate + PIX / trace * back[:, :cols], back[:, cols:]], axis=1
        )
        received = exchange(
            pushed_rows.reshape(mode_count, frames_dev, cols + EXTRA),
            "modes",
            mode_count,
            ident + 4,
        )
        squares = received[0, :, cols]
        pushed = jnp.transpose(received[:, :, :cols], (1, 0, 2)).reshape(frames_dev, -1)
        levels = jnp.sqrt(squares / trace)
        denoised, spread = lax.map(
            lambda bundle: denoise(bundle, w_first, w_mid, w_last), (pushed, levels, probe)
        )
        onsager = denoised - spread[:, None] * pushed
        gains = jnp.sum(denoised * onsager, axis=1) / (jnp.sum(onsager * onsager, axis=1) + 1e-06)
        recovered = gains[:, None] * onsager
        if iteration + 1 < ITERS:
            outgoing = jnp.transpose(recovered.reshape(frames_dev, mode_count, cols), (1, 0, 2))
            estimate = exchange(outgoing, "modes", mode_count, ident + 5).reshape(per_row, cols)
        ident += 6
    return recovered


def solution(mesh):
    return jax.shard_map(
        body,
        mesh=mesh,
        in_specs=(
            P("rows", "modes"),
            P("modes", "rows"),
            P("rows", "modes"),
            P(("rows", "modes"), None),
            P(),
            P(),
            P(),
        ),
        out_specs=P(("rows", "modes"), None),
        check_vma=False,
    )
```
